1024 devices in a mesh: row: 64 (over z, core), col: 16 (over y, x).
Axes of the slice: x: 4, y: 4, z: 32, core: 2. Of those that a mesh axis runs over, the one named last changes fastest.
Arguments:
- tensor: bfloat16 [4096, 65536], P('row', 'col'), may hold values from -6 to 6
- occ_panels: bfloat16 [1024, 8192], P(('row', 'col')), may hold values from -0.75 to 0.75
- virt_panels: bfloat16 [1024, 4096], P(('row', 'col')), may hold values from -0.75 to 0.75
- b_owner: int32 [4096, 1], P('row'), may hold values from 0 to 63; in each aligned block of 64 rows (0 to 63, 64 to 127, ...) at most 2 rows name the same one
- b_local: int32 [4096, 2], P('row'), may hold values from 0 to 15
Outputs:
- contracted: bfloat16 [4096, 131072], P('row', 'col')
The draws below stay inside these ranges and needn't reach their ends.
Inputs may be any that keep to these rules, and one draw needn't show every extreme that they name: `b_owner`: in each aligned block of 64 rows (the rows of one device) no owner appears more than 2 times, and some owner appears exactly 2 times.
All inputs are finite; a program needn't handle non-finite values.
Results may differ from the reference program's by a relative error of at most 0.0049.
Values may be sent and summed in bfloat16 or wider, within the bound.
A program may use at most 32 MiB of HBM per device.

```python
import math
import jax
import jax.numpy as jnp
import numpy as np
from jax import lax

BLK = 64
KO = 2
CAP = 2
TB = 64
NBLK = 1024
RIB = 16
N_ROW = 64
N_COL = 16


def with_ends(entries, own_key, least, top_value):
    longest = entries.shape.index(max(entries.shape))
    spots = []
    for shift in (0, 1):
        where = [jax.random.randint(jax.random.fold_in(own_key, axis), (), 0, length) for axis, length in enumerate(entries.shape)]
        where[longest] = (where[longest] + shift) % entries.shape[longest]
        spots.append(tuple(where))
    return entries.at[spots[0]].set(least).at[spots[1]].set(top_value)


def shard_levels(rng, dims, pieces, low, high):
    level = 1.0
    for position, shards_of in pieces:
        steps = jax.random.uniform(jax.random.fold_in(jax.random.fold_in(rng, 6), position), (shards_of,), jnp.float32, low / len(pieces), high / len(pieces))
        level = level * jnp.repeat(jnp.exp(steps), dims[position] // shards_of).reshape((-1,) + (1,) * (len(dims) - 1 - position))
    return level


def shared_out(stream_key, own, number, rows, amount, top, bound, slope):
    order = jax.random.permutation(stream_key, amount)
    heavy_load, ordinary = portions_of(amount, rows * top, bound, slope, True), portions_of(amount, rows * top, bound, slope, False)
    places = jnp.arange(amount)

    def named(sizes, turn):
        used = int((sizes > 0).sum())
        fixed = max(1, used // 4)
        moved = fixed + (places - fixed + turn * (used - fixed)) % max(1, amount - fixed)
        return jnp.zeros((amount,), jnp.int32).at[order[jnp.where(places < fixed, places, moved)]].set(jnp.asarray(sizes, jnp.int32))

    sizes = jnp.where(number % 4 == 0, named(heavy_load, number // 4), named(ordinary, number - number // 4 - 1))
    mixed = jax.random.permutation(jax.random.fold_in(own, 3), amount)
    giver, receiver = mixed[0:amount // 2 * 2:2], mixed[1:amount // 2 * 2:2]
    margin = jnp.minimum(sizes[giver] - 1, bound - sizes[receiver]) // 2
    margin = jnp.where((giver == order[0]) | (receiver == order[0]) | (sizes[receiver] == 0), 0, jnp.maximum(margin, 0))
    moved = jax.random.randint(jax.random.fold_in(own, 4), (amount // 2,), 0, 1 << 20) % (margin + 1)
    sizes = sizes.at[giver].add(-moved).at[receiver].add(moved)
    items = jnp.searchsorted(jnp.cumsum(sizes), jnp.arange(rows * top), side="right").astype(jnp.int32)
    grid = items.reshape(top, rows).T
    grid = grid[jax.random.permutation(jax.random.fold_in(own, 1), rows)]
    turn = jax.random.randint(jax.random.fold_in(own, 2), (rows, 1), 0, top)
    return jnp.take_along_axis(grid, (jnp.arange(top)[None, :] + turn) % top, axis=1)


def portions_of(number_of, total, limit, lean, full):
    portions = [(1 << 20) // math.isqrt(standing ** lean) + 1 for standing in range(1, number_of + 1)]
    largest = limit if full else min(limit, max(-(-total // number_of), total * portions[0] // sum(portions)))
    least = 1 if total - largest >= number_of - 1 else 0
    counts, spare = [largest] + [least] * (number_of - 1), total - largest - least * (number_of - 1)
    while spare > 0:
        movable = [i for i in range(1, number_of) if counts[i] < largest] or [i for i in range(1, number_of) if counts[i] < limit]
        mass, remaining = sum([portions[i] for i in movable]), spare
        for i in movable:
            addition = min(limit - counts[i], max(1, remaining * portions[i] // mass), spare)
            counts[i] = counts[i] + addition
            spare = spare - addition
    return np.array(counts)


def noise(rng, extent, scale, bound, cuts=(), kind=jnp.bfloat16):
    factor_of = shard_levels(rng, extent, cuts, -0.22, 0.18) if cuts else 1.0
    values = jax.random.normal(rng, extent, jnp.float32) * scale * factor_of
    return jnp.minimum(jnp.maximum(values, -bound), bound).astype(kind)


def setup_inputs(seed: int = 0) -> dict:
    seeds = jax.random.split(jax.random.key(seed), 6)
    tensor = noise(seeds[0], (N_ROW * TB, RIB * BLK * BLK), 1.0, 6.0, ((0, 64), (1, 16)))
    occ_panels = noise(seeds[1], (NBLK, KO * BLK * BLK), BLK ** -0.5, 0.75, ((0, 1024),))
    virt_panels = noise(seeds[2], (NBLK, BLK * BLK), BLK ** -0.5, 0.75, ((0, 1024),))
    b_owner_keys = jax.random.split(jax.random.fold_in(seeds[3], 1), (N_ROW * TB) // TB)
    b_owner_turns = jax.random.permutation(jax.random.fold_in(seeds[3], 3), (N_ROW * TB) // TB)
    b_owner = jax.vmap(lambda own, number: shared_out(jax.random.fold_in(seeds[3], 2), own, number, TB, N_ROW, 1, CAP, 2))(b_owner_keys, b_owner_turns).reshape((N_ROW * TB, 1))
    b_local = with_ends(jax.random.randint(seeds[4], (N_ROW * TB, 2), 0, N_COL), jax.random.fold_in(seeds[4], 1), 0, N_COL - 1).astype(jnp.int32)
    return dict(tensor=tensor, occ_panels=occ_panels, virt_panels=virt_panels, b_owner=b_owner, b_local=b_local)


def reference(tensor, occ_panels, virt_panels, b_owner, b_local):
    row_count = tensor.shape[0]
    indices = jnp.arange(row_count, dtype=jnp.int32)
    mu_block = (indices // TB) * N_COL + b_local[:, 0]
    nu_block = b_owner[:, 0] * N_COL + b_local[:, 1]
    occ_blocks = occ_panels[mu_block].reshape(row_count, BLK, KO * BLK).astype(jnp.float32)
    virt_blocks = virt_panels[nu_block].reshape(row_count, BLK, BLK).astype(jnp.float32)

    def per_column(column):
        start = (column * BLK * BLK).astype(jnp.int32)
        tiles = lax.dynamic_slice_in_dim(tensor, start, BLK * BLK, 1).reshape(row_count, BLK, BLK).astype(jnp.float32)
        middle = jnp.einsum('tnm,tmx->tnx', tiles, occ_blocks).astype(jnp.bfloat16)
        middle = lax.optimization_barrier(middle)
        output_tile = jnp.einsum('tnx,tny->txy', middle.astype(jnp.float32), virt_blocks)
        return output_tile.astype(jnp.bfloat16).reshape(row_count, KO * BLK * BLK)

    stacked = lax.map(per_column, jnp.arange(RIB, dtype=jnp.int32))
    return jnp.transpose(stacked, (1, 0, 2)).reshape(row_count, RIB * KO * BLK * BLK)
```

```python
import jax
import jax.numpy as jnp
from jax import lax
from jax.experimental import pallas as pl
from jax.experimental.pallas import tpu as pltpu
from jax.sharding import PartitionSpec as P

MESH = pl.DeviceIdType.MESH
BF = jnp.bfloat16
F32 = jnp.float32
I32 = jnp.int32

T = 64
GROUPS = 64
PLANES = 32
COLS = 16
FAR = 11
NEAR = 5
SERVED = 2 * NEAR + 1
SLOTS = 16
ENTRIES = SERVED * SLOTS
PADDED = 256
HALF = 32

NT = (((1,), (1,)), ((), ()))


def iota(shape, axis):
    return lax.broadcasted_iota(I32, shape, axis)


def one_hot(cond):
    return jnp.where(cond, 1.0, 0.0)


def dot(a, b):
    return jnp.dot(a, b, preferred_element_type=F32)


def swap_halves(v):
    return jnp.concatenate([v[:, 64:], v[:, :64]], axis=1)


def kernel(tensor, occ, virt, owner, local, local_s, out,
           tensor_v, tensor_f, occ_all, occ_t, middle, panels, far, asked, asks, replies, near, chosen,
           chosen_a, chosen_b, out_f, out_v,
           tensor_sem, out_sem,
           panel_send, panel_recv, occ_send, occ_recv, far_send, far_recv, ask_send, ask_recv,
           near_send, near_recv, last_send, last_recv):
    r, c = lax.axis_index("row"), lax.axis_index("col")
    z, core = lax.div(r, 2), lax.rem(r, 2)

    def at_plane(offset, on_core):
        return 2 * lax.rem(z + offset + PLANES, PLANES) + on_core

    def in_plane(i):
        return (r, lax.rem(c + i, COLS))

    tensor_copy = pltpu.make_async_copy(tensor, tensor_v, tensor_sem)
    tensor_copy.start()

    barrier = pltpu.get_barrier_semaphore()
    partners = [in_plane(i) for i in range(1, COLS)]
    partners += [(at_plane(o, core), c) for o in range(-NEAR, NEAR + 1) if o != 0]
    far_partners = [(at_plane(0, 1 - core), c)]
    far_partners += [(at_plane(o, lax.rem(core + k, 2)), c) for o in (-FAR, FAR) for k in (0, 1)]
    partners += far_partners
    for partner in far_partners + partners[:-len(far_partners)]:
        pl.semaphore_signal(barrier, inc=1, device_id=partner, device_id_type=MESH)

    owner_col = owner[...]
    same = iota((T, 128), 0) == iota((T, 128), 1)
    owner_row = jnp.sum(jnp.where(same, owner_col, 0), axis=0, keepdims=True)
    earlier = iota((T, 128), 1) < iota((T, 128), 0)
    rank_col = jnp.sum(jnp.where((owner_col == owner_row) & earlier, 1, 0), axis=1, keepdims=True)
    e = iota((T, PADDED), 1)
    server, w = e >> 4, e & 15
    source = w >> 2
    plane = (z + server - NEAR + FAR * (source - 1) + 2 * PLANES) & (PLANES - 1)
    group = 2 * plane + ((w >> 1) & 1)
    used = (e < ENTRIES) & (w < 12) & ((server != 0) | (source != 0))
    picks = one_hot(used & (owner_col == group) & (rank_col == (w & 1)))
    position = one_hot((iota((T, 128), 1) & 15) == local[:, 1:2]).astype(BF)
    wanted = dot(picks.T.astype(BF), position)
    row, lane = iota((PADDED, 128), 0), iota((PADDED, 128), 1)
    wanted = jnp.where(((row & 15) >> 1) == (lane >> 4), wanted, 0.0)
    asks[...] = wanted[:ENTRIES].astype(BF)
    far[96:128, :] = jnp.zeros((32, 256), BF)
    near[ENTRIES:, :] = jnp.zeros((PADDED - ENTRIES, 256), BF)

    panels[pl.ds(pl.multiple_of(c * 32, 32), 32), :] = virt[...]
    occ_all[c] = occ[...]

    pl.semaphore_wait(barrier, len(partners))

    panel_copies = []
    for i in range(1, COLS):
        rows = pl.ds(pl.multiple_of(c * 32, 32), 32)
        panel_copies.append(pltpu.make_async_remote_copy(
            virt, panels.at[rows, :], panel_send.at[i], panel_recv.at[i],
            device_id=in_plane(i), device_id_type=MESH))
        panel_copies[-1].start()
    ask_copies = []
    for k in range(SERVED):
        if k == NEAR:
            continue
        rows = pl.ds(k * SLOTS, SLOTS)
        ask_copies.append(pltpu.make_async_remote_copy(
            asks.at[rows, :], asked.at[rows, :], ask_send.at[k], ask_recv.at[k],
            device_id=(at_plane(k - NEAR, core), c), device_id_type=MESH))
        ask_copies[-1].start()
    asked[NEAR * SLOTS:(NEAR + 1) * SLOTS, :] = asks[NEAR * SLOTS:(NEAR + 1) * SLOTS, :]
    occ_copies = []
    for i in range(1, COLS):
        occ_copies.append(pltpu.make_async_remote_copy(
            occ, occ_all.at[c], occ_send.at[i], occ_recv.at[i],
            device_id=in_plane(i), device_id_type=MESH))
        occ_copies[-1].start()

    tensor_copy.wait()
    for i in range(32):
        tensor_f[i * T:(i + 1) * T, :] = tensor_v[:, i * 128:(i + 1) * 128].astype(F32)

    for copy in panel_copies:
        copy.wait()
    line, entry = iota((COLS, 512), 0), iota((COLS, 512), 1)
    held = panels[...]
    piece = [dot(one_hot((entry >> 5 == line) & ((entry & 31) == h * 16 + c)).astype(BF), held) for h in (0, 1)]
    own = pl.ds(pl.multiple_of((2 + core) * COLS, COLS), COLS)
    far[own, :] = jnp.concatenate(piece, axis=1).astype(BF)

    far_copies = []
    for n, (partner, source_there) in enumerate(zip(far_partners, (1, 2, 2, 0, 0))):
        rows = pl.ds(pl.multiple_of((2 * source_there + core) * COLS, COLS), COLS)
        far_copies.append(pltpu.make_async_remote_copy(
            far.at[own, :], far.at[rows, :], far_send.at[n], far_recv.at[n],
            device_id=partner, device_id_type=MESH))
        far_copies[-1].start()

    for copy in occ_copies:
        copy.wait()
    x_out, x_in = iota((128, 128), 0), iota((128, 128), 1)
    order = one_hot(x_in == 2 * (x_out & 63) + (x_out >> 6)).astype(BF)

    @pl.loop(0, COLS)
    def _(i):
        turned = lax.dot_general(order, occ_all[i], NT, preferred_element_type=F32)
        occ_t[i] = turned.astype(BF)

    def first(t):
        block = tensor_f[pl.ds(t, 32, stride=T), :]
        block = jnp.concatenate([block[:, :64], block[:, 64:]], axis=0).astype(BF)
        product = lax.dot_general(occ_t[local_s[t, 0]], block, NT, preferred_element_type=F32)
        middle[t] = jnp.concatenate([product[:64], product[64:]], axis=1).astype(BF)

    pl.loop(0, HALF, unroll=4)(first)

    for copy in far_copies:
        copy.wait()
    for copy in ask_copies:
        copy.wait()
    replies[...] = dot(asked[...], far[...]).astype(BF)
    near_copies = []
    for k in (0, 10, 1, 9, 2, 8, 3, 7, 4, 6):
        rows = pl.ds(k * SLOTS, SLOTS)
        near_copies.append(pltpu.make_async_remote_copy(
            replies.at[rows, :], near.at[rows, :], near_send.at[k], near_recv.at[k],
            device_id=(at_plane(NEAR - k, core), c), device_id_type=MESH))
        near_copies[-1].start()
    near[NEAR * SLOTS:(NEAR + 1) * SLOTS, :] = replies[NEAR * SLOTS:(NEAR + 1) * SLOTS, :]

    pl.loop(HALF, T, unroll=4)(first)

    for copy in near_copies:
        copy.wait()
    chosen[c] = dot(picks.astype(BF), near[...]).astype(BF)
    last_copies = []
    for h in (0, 1):
        for i in range(1, COLS):
            rows = pl.ds(h * HALF, HALF)
            last_copies.append(pltpu.make_async_remote_copy(
                chosen.at[c, rows, :], chosen.at[c, rows, :], last_send.at[h, i], last_recv.at[h, i],
                device_id=in_plane(i), device_id_type=MESH))
            last_copies[-1].start()

    low = iota((32, 128), 1) < 64
    out_copies = []
    for h in (0, 1):
        for copy in last_copies[h * 15:(h + 1) * 15]:
            copy.wait()

        @pl.loop(0, COLS)
        def _(i):
            part = chosen[i, h * HALF:(h + 1) * HALF, :].astype(F32)
            rows = pl.ds(pl.multiple_of(i * T + h * HALF, HALF), HALF)
            chosen_a[rows, :] = part[:, :128]
            chosen_b[rows, :] = part[:, 128:]

        @pl.loop(h * HALF, (h + 1) * HALF, unroll=4)
        def _(t):
            panel = jnp.concatenate(
                [chosen_a[pl.ds(t, COLS, stride=T), :], chosen_b[pl.ds(t, COLS, stride=T), :]], axis=0)
            turned = swap_halves(panel)
            both = jnp.concatenate(
                [jnp.where(low, panel, 0.0), jnp.where(low, turned, 0.0),
                 jnp.where(low, 0.0, turned), jnp.where(low, 0.0, panel)], axis=0).astype(BF)
            out_f[pl.ds(t, T, stride=T), :] = dot(middle[t], both)

        for x in range(64):
            out_v[h * HALF:(h + 1) * HALF, x * 128:(x + 1) * 128] = (
                out_f[x * T + h * HALF:x * T + (h + 1) * HALF, :].astype(BF))
        rows = pl.ds(h * HALF, HALF)
        out_copies.append(pltpu.make_async_copy(out_v.at[rows, :], out.at[rows, :], out_sem.at[h]))
        out_copies[-1].start()
    for copy in out_copies:
        copy.wait()


def on_device(tensor, occ_panels, virt_panels, b_owner, b_local):
    hbm = pl.BlockSpec(memory_space=pl.ANY)
    vmem = pl.BlockSpec(memory_space=pltpu.VMEM)
    smem = pl.BlockSpec(memory_space=pltpu.SMEM)
    dma = pltpu.SemaphoreType.DMA
    return pl.pallas_call(
        kernel,
        out_shape=jax.ShapeDtypeStruct((T, 8192), BF),
        in_specs=[hbm, vmem, vmem, vmem, vmem, smem],
        out_specs=hbm,
        scratch_shapes=[
            pltpu.VMEM((T, 4096), BF),
            pltpu.VMEM((32 * T, 128), F32),
            pltpu.VMEM((COLS, 64, 128), BF),
            pltpu.VMEM((COLS, 128, 64), BF),
            pltpu.VMEM((T, 64, 128), BF),
            pltpu.VMEM((COLS * 32, 128), BF),
            pltpu.VMEM((128, 256), BF),
            pltpu.VMEM((ENTRIES, 128), BF),
            pltpu.VMEM((ENTRIES, 128), BF),
            pltpu.VMEM((ENTRIES, 256), BF),
            pltpu.VMEM((PADDED, 256), BF),
            pltpu.VMEM((COLS, T, 256), BF),
            pltpu.VMEM((COLS * T, 128), F32),
            pltpu.VMEM((COLS * T, 128), F32),
            pltpu.VMEM((64 * T, 128), F32),
            pltpu.VMEM((T, 8192), BF),
            dma, dma((2,)),
            dma((COLS,)), dma((COLS,)), dma((COLS,)), dma((COLS,)),
            dma((6,)), dma((6,)), dma((SERVED,)), dma((SERVED,)),
            dma((SERVED,)), dma((SERVED,)), dma((2, COLS)), dma((2, COLS)),
        ],
        compiler_params=pltpu.CompilerParams(
            collective_id=0, has_side_effects=True, vmem_limit_bytes=32 << 20),
        cost_estimate=pl.CostEstimate(flops=300_000_000, bytes_accessed=3_000_000, transcendentals=0),
    )(tensor, occ_panels.reshape(64, 128), virt_panels.reshape(32, 128), b_owner, b_local, b_local)


def solution(mesh):
    placed = (
        P("row", "col"),
        P(("row", "col"), None),
        P(("row", "col"), None),
        P("row", None),
        P("row", None),
    )
    return jax.shard_map(
        on_device, mesh=mesh, in_specs=placed, out_specs=P("row", "col"), check_vma=False
    )
```

```python
import jax
import jax.numpy as jnp
from jax import lax
from jax.experimental import pallas as pl
from jax.experimental.pallas import tpu as pltpu
from jax.sharding import PartitionSpec as P

MESH = pl.DeviceIdType.MESH
BF = jnp.bfloat16
F32 = jnp.float32
I32 = jnp.int32

T = 64
GROUPS = 64
PLANES = 32
COLS = 16
FAR = 10
NEAR = 6
SERVED = 2 * NEAR + 1
SLOTS = 16
ENTRIES = SERVED * SLOTS
PADDED = 256
HALF = 32
PARTS = 2
PART = T // PARTS
STEP = 72

NT = (((1,), (1,)), ((), ()))


def iota(shape, axis):
    return lax.broadcasted_iota(I32, shape, axis)


def one_hot(cond):
    return jnp.where(cond, 1.0, 0.0)


def dot(a, b):
    return jnp.dot(a, b, preferred_element_type=F32)


def swap_halves(v):
    return jnp.concatenate([v[:, 64:], v[:, :64]], axis=1)


def kernel(tensor, occ, virt, owner, local, out,
           owner_v, local_v, local_s, occ_v, virt_v, lines,
           tensor_v, tensor_f, occ_all, occ_t, middle, panels, far, asked, asks, replies, near, chosen,
           chosen_f, out_f,
           in_sem, relay,
           panel_send, panel_recv, occ_send, occ_recv, far_send, far_recv, ask_send, ask_recv,
           near_send, near_recv, even_send, even_recv, odd_send, odd_recv):
    r, c = lax.axis_index("row"), lax.axis_index("col")
    z, core = lax.div(r, 2), lax.rem(r, 2)

    def at_plane(offset, on_core):
        return 2 * lax.rem(z + offset + PLANES, PLANES) + on_core

    def in_plane(i):
        return (r, lax.rem(c + i, COLS))

    def send(source, target, send_sem, recv_sem, partner):
        copy = pltpu.make_async_remote_copy(source, target, send_sem, recv_sem,
                                            device_id=partner, device_id_type=MESH)
        copy.start()
        return copy

    in_copies = [
        pltpu.make_async_copy(source, target, in_sem.at[n]) for n, (source, target) in enumerate(
            ((virt, virt_v), (occ, occ_v), (owner, owner_v), (local, local_v), (local, local_s), (tensor, tensor_v)))]
    for copy in in_copies:
        copy.start()
    virt_copy, occ_copy, owner_copy, local_copy, scalar_copy, tensor_copy = in_copies

    barrier = pltpu.get_barrier_semaphore()
    other = (at_plane(0, 1 - core), c)
    relays = [(at_plane(o, lax.rem(core + k, 2)), c) for o in (-NEAR, NEAR) for k in (0, 1)]
    partners = relays + [(at_plane(o, core), c) for o in range(1 - NEAR, NEAR) if o != 0]
    partners += [in_plane(i) for i in range(1, COLS)] + [other]
    far_partners = [(at_plane(o, lax.rem(core + k, 2)), c) for o in (-FAR, FAR) for k in (0, 1)] + [other]
    for partner in partners:
        pl.semaphore_signal(barrier, inc=1, device_id=partner, device_id_type=MESH)

    my_panel = pl.ds(pl.multiple_of(c * 32, 32), 32)
    virt_copy.wait()
    for i in range(32):
        lines[i:i + 1, :] = virt_v[:, i * 128:(i + 1) * 128].astype(F32)
    panels[my_panel, :] = lines[:32, :].astype(BF)
    line, entry = iota((COLS, 512), 0), iota((COLS, 512), 1)
    takes = [one_hot((entry >> 5 == line) & ((entry & 31) == h * 16 + c)).astype(BF) for h in (0, 1)]

    pl.semaphore_wait(barrier, len(partners))

    panel_copies = [send(panels.at[my_panel, :], panels.at[my_panel, :], panel_send.at[i], panel_recv.at[i],
                         in_plane(i)) for i in range(1, COLS)]
    for n, partner in enumerate(relays):
        pl.semaphore_signal(relay.at[n], inc=1, device_id=partner, device_id_type=MESH)
    occ_copy.wait()
    for i in range(64):
        lines[i:i + 1, :] = occ_v[:, i * 128:(i + 1) * 128].astype(F32)
    occ_all[c] = lines[...].astype(BF)

    owner_copy.wait()
    local_copy.wait()
    same = iota((T, T), 0) == iota((T, T), 1)
    owner_row = owner_v[...]
    owner_col = jnp.sum(jnp.where(same, owner_row, 0), axis=1, keepdims=True)
    local_col = jnp.sum(jnp.where(same, local_v[1:2, :], 0), axis=1, keepdims=True)
    earlier = iota((T, T), 1) < iota((T, T), 0)
    rank_col = jnp.sum(jnp.where((owner_col == owner_row) & earlier, 1, 0), axis=1, keepdims=True)
    e = iota((T, PADDED), 1)
    server, w = e >> 4, e & 15
    source = w >> 2
    away = server - NEAR + FAR * (source - 1)
    plane = (z + away + 2 * PLANES) & (PLANES - 1)
    group = 2 * plane + ((w >> 1) & 1)
    used = (e < ENTRIES) & (w < 12) & ((source == 1) | (away > NEAR) | ((away < -NEAR) & (away > -PLANES // 2)))
    picks = one_hot(used & (owner_col == group) & (rank_col == (w & 1)))
    position = one_hot((iota((T, 128), 1) & 15) == local_col).astype(BF)
    wanted = dot(picks.T.astype(BF), position)
    row, lane = iota((PADDED, 128), 0), iota((PADDED, 128), 1)
    wanted = jnp.where(((row & 15) >> 1) == (lane >> 4), wanted, 0.0)
    asks[...] = wanted[:ENTRIES].astype(BF)
    picks = picks.astype(BF)
    served = [k for k in range(SERVED) if k != NEAR]
    served.sort(key=lambda k: -abs(k - NEAR))
    mine = slice(NEAR * SLOTS, (NEAR + 1) * SLOTS)
    ask_copies = []
    for k in served:
        rows = pl.ds(k * SLOTS, SLOTS)
        ask_copies.append(send(asks.at[rows, :], asked.at[rows, :], ask_send.at[k], ask_recv.at[k],
                               (at_plane(k - NEAR, core), c)))
    asked[mine, :] = asks[mine, :]
    for h in (0, 1):
        far[h, 96:128, :] = jnp.zeros((32, 128), BF)
        near[h, ENTRIES:, :] = jnp.zeros((PADDED - ENTRIES, 128), BF)

    tensor_copy.wait()
    for i in range(32):
        tensor_f[i * STEP:i * STEP + T, :] = tensor_v[:, i * 128:(i + 1) * 128].astype(F32)

    for copy in panel_copies:
        copy.wait()
    for n in range(len(relays)):
        pl.semaphore_wait(relay.at[n], 1)

    own = pl.ds(pl.multiple_of((2 + core) * COLS, COLS), COLS)
    far_copies = []
    for h in (0, 1):
        far[h, own, :] = dot(takes[h], panels[...]).astype(BF)
        for n, (partner, source_there) in enumerate(zip(far_partners, (2, 2, 0, 0, 1))):
            rows = pl.ds(pl.multiple_of((2 * source_there + core) * COLS, COLS), COLS)
            far_copies.append(send(far.at[h, own, :], far.at[h, rows, :], far_send.at[h, n], far_recv.at[h, n],
                                   partner))

    occ_copies = [send(occ_all.at[c], occ_all.at[c], occ_send.at[i], occ_recv.at[i], in_plane(i))
                  for i in range(1, COLS)]

    for copy in ask_copies:
        copy.wait()
    near_copies = []
    for h in (0, 1):
        for copy in far_copies[h * 5:(h + 1) * 5]:
            copy.wait()
        replies[h] = dot(asked[...], far[h]).astype(BF)
        for k in served:
            rows = pl.ds(k * SLOTS, SLOTS)
            near_copies.append(send(replies.at[h, rows, :], near.at[h, rows, :], near_send.at[h, k],
                                    near_recv.at[h, k], (at_plane(NEAR - k, core), c)))
        near[h, mine, :] = replies[h, mine, :]

    for copy in occ_copies:
        copy.wait()
    scalar_copy.wait()
    x_out, x_in = iota((128, 128), 0), iota((128, 128), 1)
    order = one_hot(x_in == 2 * (x_out & 63) + (x_out >> 6)).astype(BF)

    @pl.loop(0, COLS, unroll=4)
    def _(i):
        turned = lax.dot_general(order, occ_all[i], NT, preferred_element_type=F32)
        occ_t[i] = turned.astype(BF)

    def first(t):
        block = tensor_f[pl.ds(t, 32, stride=STEP), :]
        block = jnp.concatenate([block[:, :64], block[:, 64:]], axis=0).astype(BF)
        product = lax.dot_general(occ_t[local_s[0, t]], block, NT, preferred_element_type=F32)
        middle[t] = jnp.concatenate([product[:64], product[64:]], axis=1).astype(BF)

    pl.loop(0, T, unroll=8)(first)

    n_near = len(served)
    for copy in near_copies[:n_near]:
        copy.wait()
    chosen[0, c] = dot(picks, near[0]).astype(BF)
    even_copies = [send(chosen.at[0, c], chosen.at[0, c], even_send.at[i], even_recv.at[i], in_plane(i))
                   for i in range(1, COLS)]
    for copy in near_copies[n_near:]:
        copy.wait()
    chosen[1, c] = dot(picks, near[1]).astype(BF)
    odd_copies = []
    for p in range(PARTS):
        rows = pl.ds(p * PART, PART)
        odd_copies += [send(chosen.at[1, c, rows, :], chosen.at[1, c, rows, :], odd_send.at[p, i], odd_recv.at[p, i],
                            in_plane(i)) for i in range(1, COLS)]

    low = iota((32, 128), 1) < 64

    def second(t):
        panel = jnp.concatenate([chosen_f[h, pl.ds(t, COLS, stride=STEP), :] for h in (0, 1)], axis=0)
        turned = swap_halves(panel)
        both = jnp.concatenate(
            [jnp.where(low, panel, 0.0), jnp.where(low, turned, 0.0),
             jnp.where(low, 0.0, turned), jnp.where(low, 0.0, panel)], axis=0).astype(BF)
        out_f[pl.ds(t, T, stride=STEP), :] = dot(middle[t], both)

    for copy in even_copies:
        copy.wait()
    for i in range(COLS):
        chosen_f[0, i * STEP:i * STEP + T, :] = chosen[0, i].astype(F32)
    for p in range(PARTS):
        for copy in odd_copies[p * 15:(p + 1) * 15]:
            copy.wait()
        for i in range(COLS):
            chosen_f[1, i * STEP + p * PART:i * STEP + (p + 1) * PART, :] = (
                chosen[1, i, p * PART:(p + 1) * PART, :].astype(F32))
        pl.loop(p * PART, (p + 1) * PART, unroll=16)(second)
        for x in range(64):
            out[p * PART:(p + 1) * PART, x * 128:(x + 1) * 128] = (
                out_f[x * STEP + p * PART:x * STEP + (p + 1) * PART, :].astype(BF))


def on_device(tensor, occ_panels, virt_panels, b_owner, b_local):
    hbm = pl.BlockSpec(memory_space=pltpu.HBM)
    operands = (tensor, occ_panels, virt_panels, b_owner.T, b_local.T)
    operands = [pltpu.with_memory_space_constraint(operand, pltpu.HBM) for operand in operands]
    dma = pltpu.SemaphoreType.DMA
    return pl.pallas_call(
        kernel,
        out_shape=pltpu.VMEM((T, 8192), BF),
        in_specs=[hbm] * 5,
        out_specs=pl.BlockSpec(memory_space=pltpu.VMEM),
        scratch_shapes=[
            pltpu.VMEM((1, T), I32),
            pltpu.VMEM((2, T), I32),
            pltpu.SMEM((2, T), I32),
            pltpu.VMEM((1, 8192), BF),
            pltpu.VMEM((1, 4096), BF),
            pltpu.VMEM((64, 128), F32),
            pltpu.VMEM((T, 4096), BF),
            pltpu.VMEM((32 * STEP, 128), F32),
            pltpu.VMEM((COLS, 64, 128), BF),
            pltpu.VMEM((COLS, 128, 64), BF),
            pltpu.VMEM((T, 64, 128), BF),
            pltpu.VMEM((COLS * 32, 128), BF),
            pltpu.VMEM((2, 128, 128), BF),
            pltpu.VMEM((ENTRIES, 128), BF),
            pltpu.VMEM((ENTRIES, 128), BF),
            pltpu.VMEM((2, ENTRIES, 128), BF),
            pltpu.VMEM((2, PADDED, 128), BF),
            pltpu.VMEM((2, COLS, T, 128), BF),
            pltpu.VMEM((2, COLS * STEP, 128), F32),
            pltpu.VMEM((64 * STEP, 128), F32),
            dma((6,)), pltpu.SemaphoreType.REGULAR((4,)),
            dma((COLS,)), dma((COLS,)), dma((COLS,)), dma((COLS,)),
            dma((2, 5)), dma((2, 5)), dma((SERVED,)), dma((SERVED,)),
            dma((2, SERVED)), dma((2, SERVED)),
            dma((COLS,)), dma((COLS,)), dma((PARTS, COLS)), dma((PARTS, COLS)),
        ],
        compiler_params=pltpu.CompilerParams(
            collective_id=0, has_side_effects=True, vmem_limit_bytes=32 << 20),
        cost_estimate=pl.CostEstimate(flops=300_000_000, bytes_accessed=3_000_000, transcendentals=0),
    )(*operands)


def solution(mesh):
    placed = (
        P("row", "col"),
        P(("row", "col"), None),
        P(("row", "col"), None),
        P("row", None),
        P("row", None),
    )
    return jax.shard_map(
        on_device, mesh=mesh, in_specs=placed, out_specs=P("row", "col"), check_vma=False
    )
```

```python
import jax
import jax.numpy as jnp
from jax import lax
from jax.experimental import pallas as pl
from jax.experimental.pallas import tpu as pltpu
from jax.sharding import PartitionSpec as P

MESH = pl.DeviceIdType.MESH
BF = jnp.bfloat16
F32 = jnp.float32
I32 = jnp.int32

T = 64
PLANES = 32
SIDE = 4
COLS = 16
FAR = 10
NEAR = 6
STAGE = FAR - NEAR
SERVED = 2 * NEAR + 1
SLOTS = 16
ENTRIES = SERVED * SLOTS
PADDED = 256
HALF = 32
PARTS = 2
PART = T // PARTS
STEP = 72


def hops(i):
    return min(i // SIDE, SIDE - i // SIDE) + min(i % SIDE, SIDE - i % SIDE)


NEIGHBOURS = sorted(range(1, COLS), key=lambda i: -hops(i))

NT = (((1,), (1,)), ((), ()))


def iota(shape, axis):
    return lax.broadcasted_iota(I32, shape, axis)


def one_hot(cond):
    return jnp.where(cond, 1.0, 0.0)


def dot(a, b):
    return jnp.dot(a, b, preferred_element_type=F32)


def swap_halves(v):
    return jnp.concatenate([v[:, 64:], v[:, :64]], axis=1)


def kernel(tensor, occ, virt, owner, local, out,
           owner_v, local_v, local_s, occ_v, virt_v, lines,
           tensor_v, tensor_f, occ_all, occ_t, middle, cuts, pieces, far, asked, asks, replies, near, chosen,
           chosen_f, out_f,
           in_sem, relay,
           panel_send, panel_recv, occ_send, occ_recv, far_send, far_recv, ask_send, ask_recv,
           near_send, near_recv, even_send, even_recv, odd_send, odd_recv):
    r, c = lax.axis_index("row"), lax.axis_index("col")
    z, core = lax.div(r, 2), lax.rem(r, 2)

    def at_plane(offset, on_core):
        return 2 * lax.rem(z + offset + PLANES, PLANES) + on_core

    line, place = lax.div(c, SIDE), lax.rem(c, SIDE)

    def in_plane(i):
        dy, dx = i // SIDE, i % SIDE
        return (r, SIDE * lax.rem(line + dy, SIDE) + lax.rem(place + dx, SIDE))

    def send(source, target, send_sem, recv_sem, partner):
        copy = pltpu.make_async_remote_copy(source, target, send_sem, recv_sem,
                                            device_id=partner, device_id_type=MESH)
        copy.start()
        return copy

    in_copies = [
        pltpu.make_async_copy(source, target, in_sem.at[n]) for n, (source, target) in enumerate(
            ((virt, virt_v), (occ, occ_v), (owner, owner_v), (local, local_v), (local, local_s), (tensor, tensor_v)))]
    virt_copy, occ_copy, owner_copy, local_copy, scalar_copy, tensor_copy = in_copies
    virt_copy.start()

    barrier = pltpu.get_barrier_semaphore()
    other = (at_plane(0, 1 - core), c)
    relays = [(at_plane(o, lax.rem(core + k, 2)), c) for o in (-STAGE, STAGE) for k in (0, 1)]
    far_partners = [(at_plane(o, lax.rem(core + k, 2)), c) for o in (-FAR, FAR) for k in (0, 1)] + [other]
    partners = [(STAGE, partner) for partner in relays] + [(0, other)]
    partners += [(abs(o), (at_plane(o, core), c)) for o in range(-NEAR, NEAR + 1) if o not in (0, STAGE, -STAGE)]
    partners += [(hops(i), in_plane(i)) for i in NEIGHBOURS]
    for _, partner in sorted(partners, key=lambda pair: -pair[0]):
        pl.semaphore_signal(barrier, inc=1, device_id=partner, device_id_type=MESH)
    for copy in in_copies[1:]:
        copy.start()

    virt_copy.wait()
    for i in range(32):
        cuts[i % COLS, i // COLS:i // COLS + 1, :] = virt_v[:, i * 128:(i + 1) * 128].astype(F32)
    pieces[c] = cuts[c]

    pl.semaphore_wait(barrier, len(partners))

    for n, partner in enumerate(relays):
        pl.semaphore_signal(relay.at[n], inc=1, device_id=partner, device_id_type=MESH)
    panel_copies = []
    for i in NEIGHBOURS:
        partner = in_plane(i)
        panel_copies.append(send(cuts.at[partner[1]], pieces.at[c], panel_send.at[i], panel_recv.at[i], partner))
    occ_copy.wait()
    for i in range(64):
        lines[i:i + 1, :] = occ_v[:, i * 128:(i + 1) * 128].astype(F32)
    occ_all[c] = lines[...].astype(BF)

    owner_copy.wait()
    local_copy.wait()
    same = iota((T, T), 0) == iota((T, T), 1)
    owner_row = owner_v[...]
    owner_col = jnp.sum(jnp.where(same, owner_row, 0), axis=1, keepdims=True)
    local_col = jnp.sum(jnp.where(same, local_v[1:2, :], 0), axis=1, keepdims=True)
    earlier = iota((T, T), 1) < iota((T, T), 0)
    rank_col = jnp.sum(jnp.where((owner_col == owner_row) & earlier, 1, 0), axis=1, keepdims=True)
    e = iota((T, PADDED), 1)
    server, w = e >> 4, e & 15
    source = w >> 2
    away = server - NEAR + FAR * (source - 1)
    plane = (z + away + 2 * PLANES) & (PLANES - 1)
    group = 2 * plane + ((w >> 1) & 1)
    used = (e < ENTRIES) & (w < 12) & ((source == 1) | (away > NEAR) | ((away < -NEAR) & (away > -PLANES // 2)))
    picks = one_hot(used & (owner_col == group) & (rank_col == (w & 1)))
    position = one_hot((iota((T, 128), 1) & 15) == local_col).astype(BF)
    wanted = dot(picks.T.astype(BF), position)
    row, lane = iota((PADDED, 128), 0), iota((PADDED, 128), 1)
    wanted = jnp.where(((row & 15) >> 1) == (lane >> 4), wanted, 0.0)
    asks[...] = wanted[:ENTRIES].astype(BF)
    picks = picks.astype(BF)
    served = [k for k in range(SERVED) if k != NEAR]
    served.sort(key=lambda k: -abs(k - NEAR))
    mine = slice(NEAR * SLOTS, (NEAR + 1) * SLOTS)
    ask_copies = []
    for k in served:
        rows = pl.ds(k * SLOTS, SLOTS)
        ask_copies.append(send(asks.at[rows, :], asked.at[rows, :], ask_send.at[k], ask_recv.at[k],
                               (at_plane(k - NEAR, core), c)))
    asked[mine, :] = asks[mine, :]
    for h in (0, 1):
        far[h, 96:128, :] = jnp.zeros((32, 128), BF)
        near[h, ENTRIES:, :] = jnp.zeros((PADDED - ENTRIES, 128), BF)

    tensor_copy.wait()
    for i in range(32):
        tensor_f[i * STEP:i * STEP + T, :] = tensor_v[:, i * 128:(i + 1) * 128].astype(F32)

    for copy in panel_copies:
        copy.wait()
    for n in range(len(relays)):
        pl.semaphore_wait(relay.at[n], 1)

    own = pl.ds(pl.multiple_of((2 + core) * COLS, COLS), COLS)
    far_copies = []
    for h in (0, 1):
        far[h, own, :] = pieces[:, h, :].astype(BF)
        for n, (partner, source_there) in enumerate(zip(far_partners, (2, 2, 0, 0, 1))):
            rows = pl.ds(pl.multiple_of((2 * source_there + core) * COLS, COLS), COLS)
            far_copies.append(send(far.at[h, own, :], far.at[h, rows, :], far_send.at[h, n], far_recv.at[h, n],
                                   partner))

    occ_copies = [send(occ_all.at[c], occ_all.at[c], occ_send.at[i], occ_recv.at[i], in_plane(i))
                  for i in NEIGHBOURS]

    for copy in ask_copies:
        copy.wait()
    near_copies = []
    for h in (0, 1):
        for copy in far_copies[h * 5:(h + 1) * 5]:
            copy.wait()
        replies[h] = dot(asked[...], far[h]).astype(BF)
        for k in served:
            rows = pl.ds(k * SLOTS, SLOTS)
            near_copies.append(send(replies.at[h, rows, :], near.at[h, rows, :], near_send.at[h, k],
                                    near_recv.at[h, k], (at_plane(NEAR - k, core), c)))
        near[h, mine, :] = replies[h, mine, :]

    for copy in occ_copies:
        copy.wait()
    scalar_copy.wait()
    x_out, x_in = iota((128, 128), 0), iota((128, 128), 1)
    order = one_hot(x_in == 2 * (x_out & 63) + (x_out >> 6)).astype(BF)

    @pl.loop(0, COLS, unroll=4)
    def _(i):
        turned = lax.dot_general(order, occ_all[i], NT, preferred_element_type=F32)
        occ_t[i] = turned.astype(BF)

    def first(t):
        block = tensor_f[pl.ds(t, 32, stride=STEP), :]
        block = jnp.concatenate([block[:, :64], block[:, 64:]], axis=0).astype(BF)
        product = lax.dot_general(occ_t[local_s[0, t]], block, NT, preferred_element_type=F32)
        middle[t] = jnp.concatenate([product[:64], product[64:]], axis=1).astype(BF)

    pl.loop(0, T, unroll=8)(first)

    n_near = len(served)
    for copy in near_copies[:n_near]:
        copy.wait()
    chosen[0, c] = dot(picks, near[0]).astype(BF)
    even_copies = [send(chosen.at[0, c], chosen.at[0, c], even_send.at[i], even_recv.at[i], in_plane(i))
                   for i in NEIGHBOURS]
    for copy in near_copies[n_near:]:
        copy.wait()
    chosen[1, c] = dot(picks, near[1]).astype(BF)
    odd_copies = []
    for p in range(PARTS):
        rows = pl.ds(p * PART, PART)
        odd_copies += [send(chosen.at[1, c, rows, :], chosen.at[1, c, rows, :], odd_send.at[p, i], odd_recv.at[p, i],
                            in_plane(i)) for i in NEIGHBOURS]

    low = iota((32, 128), 1) < 64

    def second(t):
        panel = jnp.concatenate([chosen_f[h, pl.ds(t, COLS, stride=STEP), :] for h in (0, 1)], axis=0)
        turned = swap_halves(panel)
        both = jnp.concatenate(
            [jnp.where(low, panel, 0.0), jnp.where(low, turned, 0.0),
             jnp.where(low, 0.0, turned), jnp.where(low, 0.0, panel)], axis=0).astype(BF)
        out_f[pl.ds(t, T, stride=STEP), :] = dot(middle[t], both)

    for copy in even_copies:
        copy.wait()
    for i in range(COLS):
        chosen_f[0, i * STEP:i * STEP + T, :] = chosen[0, i].astype(F32)
    for p in range(PARTS):
        for copy in odd_copies[p * 15:(p + 1) * 15]:
            copy.wait()
        for i in range(COLS):
            chosen_f[1, i * STEP + p * PART:i * STEP + (p + 1) * PART, :] = (
                chosen[1, i, p * PART:(p + 1) * PART, :].astype(F32))
        pl.loop(p * PART, (p + 1) * PART, unroll=16)(second)
        for x in range(64):
            out[p * PART:(p + 1) * PART, x * 128:(x + 1) * 128] = (
                out_f[x * STEP + p * PART:x * STEP + (p + 1) * PART, :].astype(BF))


def on_device(tensor, occ_panels, virt_panels, b_owner, b_local):
    hbm = pl.BlockSpec(memory_space=pltpu.HBM)
    operands = (tensor, occ_panels, virt_panels, b_owner.T, b_local.T)
    operands = [pltpu.with_memory_space_constraint(operand, pltpu.HBM) for operand in operands]
    dma = pltpu.SemaphoreType.DMA
    return pl.pallas_call(
        kernel,
        out_shape=pltpu.VMEM((T, 8192), BF),
        in_specs=[hbm] * 5,
        out_specs=pl.BlockSpec(memory_space=pltpu.VMEM),
        scratch_shapes=[
            pltpu.VMEM((1, T), I32),
            pltpu.VMEM((2, T), I32),
            pltpu.SMEM((2, T), I32),
            pltpu.VMEM((1, 8192), BF),
            pltpu.VMEM((1, 4096), BF),
            pltpu.VMEM((64, 128), F32),
            pltpu.VMEM((T, 4096), BF),
            pltpu.VMEM((33 * STEP, 128), F32),
            pltpu.VMEM((COLS, 64, 128), BF),
            pltpu.VMEM((COLS, 128, 64), BF),
            pltpu.VMEM((T, 64, 128), BF),
            pltpu.VMEM((COLS, 2, 128), F32),
            pltpu.VMEM((COLS, 2, 128), F32),
            pltpu.VMEM((2, 128, 128), BF),
            pltpu.VMEM((ENTRIES, 128), BF),
            pltpu.VMEM((ENTRIES, 128), BF),
            pltpu.VMEM((2, ENTRIES, 128), BF),
            pltpu.VMEM((2, PADDED, 128), BF),
            pltpu.VMEM((2, COLS, T, 128), BF),
            pltpu.VMEM((2, (COLS + 1) * STEP, 128), F32),
            pltpu.VMEM((65 * STEP, 128), F32),
            dma((6,)), pltpu.SemaphoreType.REGULAR((4,)),
            dma((COLS,)), dma((COLS,)), dma((COLS,)), dma((COLS,)),
            dma((2, 5)), dma((2, 5)), dma((SERVED,)), dma((SERVED,)),
            dma((2, SERVED)), dma((2, SERVED)),
            dma((COLS,)), dma((COLS,)), dma((PARTS, COLS)), dma((PARTS, COLS)),
        ],
        compiler_params=pltpu.CompilerParams(
            collective_id=0, has_side_effects=True, vmem_limit_bytes=32 << 20),
        cost_estimate=pl.CostEstimate(flops=300_000_000, bytes_accessed=3_000_000, transcendentals=0),
    )(*operands)


def solution(mesh):
    placed = (
        P("row", "col"),
        P(("row", "col"), None),
        P(("row", "col"), None),
        P("row", None),
        P("row", None),
    )
    return jax.shard_map(
        on_device, mesh=mesh, in_specs=placed, out_specs=P("row", "col"), check_vma=False
    )
```

```python
import jax
import jax.numpy as jnp
from jax import lax
from jax.experimental import pallas as pl
from jax.experimental.pallas import tpu as pltpu
from jax.sharding import PartitionSpec as P

MESH = pl.DeviceIdType.MESH
BF = jnp.bfloat16
F32 = jnp.float32
I32 = jnp.int32

T = 64
PLANES = 32
SIDE = 4
COLS = 16
FAR = 10
NEAR = 6
STAGE = FAR - NEAR
SERVED = 2 * NEAR + 1
SLOTS = 16
ENTRIES = SERVED * SLOTS
PADDED = 256
HALF = 32
PARTS = 2
PART = T // PARTS
STEP = 72


def hops(i):
    return min(i // SIDE, SIDE - i // SIDE) + min(i % SIDE, SIDE - i % SIDE)


NEIGHBOURS = sorted(range(1, COLS), key=lambda i: -hops(i))

NT = (((1,), (1,)), ((), ()))


def iota(shape, axis):
    return lax.broadcasted_iota(I32, shape, axis)


def one_hot(cond):
    return jnp.where(cond, 1.0, 0.0)


def dot(a, b):
    return jnp.dot(a, b, preferred_element_type=F32)


def swap_halves(v):
    return jnp.concatenate([v[:, 64:], v[:, :64]], axis=1)


def kernel(tensor, occ, virt, owner, local, out,
           owner_v, local_v, local_s, occ_v, virt_v, lines,
           tensor_v, tensor_f, occ_all, occ_t, middle, cuts, pieces, far, asked, asks, replies, near, chosen,
           chosen_f, out_f,
           in_sem, relay,
           panel_send, panel_recv, occ_send, occ_recv, far_send, far_recv, ask_send, ask_recv,
           near_send, near_recv, even_send, even_recv, odd_send, odd_recv):
    r, c = lax.axis_index("row"), lax.axis_index("col")
    z, core = lax.div(r, 2), lax.rem(r, 2)

    def at_plane(offset, on_core):
        return 2 * lax.rem(z + offset + PLANES, PLANES) + on_core

    line, place = lax.div(c, SIDE), lax.rem(c, SIDE)

    def in_plane(i):
        dy, dx = i // SIDE, i % SIDE
        return (r, SIDE * lax.rem(line + dy, SIDE) + lax.rem(place + dx, SIDE))

    def send(source, target, send_sem, recv_sem, partner):
        copy = pltpu.make_async_remote_copy(source, target, send_sem, recv_sem,
                                            device_id=partner, device_id_type=MESH)
        copy.start()
        return copy

    in_copies = [
        pltpu.make_async_copy(source, target, in_sem.at[n]) for n, (source, target) in enumerate(
            ((virt, virt_v), (occ, occ_v), (owner, owner_v), (local, local_v), (local, local_s), (tensor, tensor_v)))]
    virt_copy, occ_copy, owner_copy, local_copy, scalar_copy, tensor_copy = in_copies
    virt_copy.start()

    barrier = pltpu.get_barrier_semaphore()
    other = (at_plane(0, 1 - core), c)
    relays = [(at_plane(o, lax.rem(core + k, 2)), c) for o in (-STAGE, STAGE) for k in (0, 1)]
    far_partners = [(at_plane(o, lax.rem(core + k, 2)), c) for o in (-FAR, FAR) for k in (0, 1)] + [other]
    partners = [(STAGE, partner) for partner in relays] + [(0, other)]
    partners += [(abs(o), (at_plane(o, core), c)) for o in range(-NEAR, NEAR + 1) if o not in (0, STAGE, -STAGE)]
    partners += [(hops(i), in_plane(i)) for i in NEIGHBOURS]
    for _, partner in sorted(partners, key=lambda pair: -pair[0]):
        pl.semaphore_signal(barrier, inc=1, device_id=partner, device_id_type=MESH)
    for copy in in_copies[1:]:
        copy.start()

    virt_copy.wait()
    for i in range(32):
        cuts[i % COLS, i // COLS:i // COLS + 1, :] = virt_v[:, i * 128:(i + 1) * 128].astype(F32)
    pieces[c] = cuts[c]

    pl.semaphore_wait(barrier, len(partners))

    for n, partner in enumerate(relays):
        pl.semaphore_signal(relay.at[n], inc=1, device_id=partner, device_id_type=MESH)
    panel_copies = []
    for i in NEIGHBOURS:
        partner = in_plane(i)
        panel_copies.append(send(cuts.at[partner[1]], pieces.at[c], panel_send.at[i], panel_recv.at[i], partner))

    owner_copy.wait()
    local_copy.wait()
    same = iota((T, T), 0) == iota((T, T), 1)
    owner_row = owner_v[...]
    owner_col = jnp.sum(jnp.where(same, owner_row, 0), axis=1, keepdims=True)
    local_col = jnp.sum(jnp.where(same, local_v[1:2, :], 0), axis=1, keepdims=True)
    earlier = iota((T, T), 1) < iota((T, T), 0)
    rank_col = jnp.sum(jnp.where((owner_col == owner_row) & earlier, 1, 0), axis=1, keepdims=True)
    e = iota((T, PADDED), 1)
    server, w = e >> 4, e & 15
    source = w >> 2
    away = server - NEAR + FAR * (source - 1)
    plane = (z + away + 2 * PLANES) & (PLANES - 1)
    group = 2 * plane + ((w >> 1) & 1)
    used = (e < ENTRIES) & (w < 12) & ((source == 1) | (away > NEAR) | ((away < -NEAR) & (away > -PLANES // 2)))
    picks = one_hot(used & (owner_col == group) & (rank_col == (w & 1)))
    position = one_hot((iota((T, 128), 1) & 15) == local_col).astype(BF)
    wanted = dot(picks.T.astype(BF), position)
    row, lane = iota((PADDED, 128), 0), iota((PADDED, 128), 1)
    wanted = jnp.where(((row & 15) >> 1) == (lane >> 4), wanted, 0.0)
    asks[...] = wanted[:ENTRIES].astype(BF)
    picks = picks.astype(BF)
    served = [k for k in range(SERVED) if k != NEAR]
    served.sort(key=lambda k: -abs(k - NEAR))
    mine = slice(NEAR * SLOTS, (NEAR + 1) * SLOTS)
    ask_copies = []
    for k in served:
        rows = pl.ds(k * SLOTS, SLOTS)
        ask_copies.append(send(asks.at[rows, :], asked.at[rows, :], ask_send.at[k], ask_recv.at[k],
                               (at_plane(k - NEAR, core), c)))
    asked[mine, :] = asks[mine, :]
    for h in (0, 1):
        far[h, 96:128, :] = jnp.zeros((32, 128), BF)
        near[h, ENTRIES:, :] = jnp.zeros((PADDED - ENTRIES, 128), BF)

    for copy in panel_copies:
        copy.wait()
    for n in range(len(relays)):
        pl.semaphore_wait(relay.at[n], 1)

    own = pl.ds(pl.multiple_of((2 + core) * COLS, COLS), COLS)
    far_copies = []
    for h in (0, 1):
        far[h, own, :] = pieces[:, h, :].astype(BF)
        for n, (partner, source_there) in enumerate(zip(far_partners, (2, 2, 0, 0, 1))):
            rows = pl.ds(pl.multiple_of((2 * source_there + core) * COLS, COLS), COLS)
            far_copies.append(send(far.at[h, own, :], far.at[h, rows, :], far_send.at[h, n], far_recv.at[h, n],
                                   partner))

    occ_copy.wait()
    for i in range(64):
        lines[i:i + 1, :] = occ_v[:, i * 128:(i + 1) * 128].astype(F32)
    occ_all[c] = lines[...].astype(BF)
    occ_copies = [send(occ_all.at[c], occ_all.at[c], occ_send.at[i], occ_recv.at[i], in_plane(i))
                  for i in NEIGHBOURS]

    tensor_copy.wait()
    for i in range(32):
        tensor_f[i * STEP:i * STEP + T, :] = tensor_v[:, i * 128:(i + 1) * 128].astype(F32)

    for copy in ask_copies:
        copy.wait()
    near_copies = []
    for h in (0, 1):
        for copy in far_copies[h * 5:(h + 1) * 5]:
            copy.wait()
        replies[h] = dot(asked[...], far[h]).astype(BF)
        for k in served:
            rows = pl.ds(k * SLOTS, SLOTS)
            near_copies.append(send(replies.at[h, rows, :], near.at[h, rows, :], near_send.at[h, k],
                                    near_recv.at[h, k], (at_plane(NEAR - k, core), c)))
        near[h, mine, :] = replies[h, mine, :]

    for copy in occ_copies:
        copy.wait()
    scalar_copy.wait()
    x_out, x_in = iota((128, 128), 0), iota((128, 128), 1)
    order = one_hot(x_in == 2 * (x_out & 63) + (x_out >> 6)).astype(BF)

    @pl.loop(0, COLS, unroll=4)
    def _(i):
        turned = lax.dot_general(order, occ_all[i], NT, preferred_element_type=F32)
        occ_t[i] = turned.astype(BF)

    def first(t):
        block = tensor_f[pl.ds(t, 32, stride=STEP), :]
        block = jnp.concatenate([block[:, :64], block[:, 64:]], axis=0).astype(BF)
        product = lax.dot_general(occ_t[local_s[0, t]], block, NT, preferred_element_type=F32)
        middle[t] = jnp.concatenate([product[:64], product[64:]], axis=1).astype(BF)

    pl.loop(0, T, unroll=8)(first)

    n_near = len(served)
    for copy in near_copies[:n_near]:
        copy.wait()
    chosen[0, c] = dot(picks, near[0]).astype(BF)
    even_copies = [send(chosen.at[0, c], chosen.at[0, c], even_send.at[i], even_recv.at[i], in_plane(i))
                   for i in NEIGHBOURS]
    for copy in near_copies[n_near:]:
        copy.wait()
    chosen[1, c] = dot(picks, near[1]).astype(BF)
    odd_copies = []
    for p in range(PARTS):
        rows = pl.ds(p * PART, PART)
        odd_copies += [send(chosen.at[1, c, rows, :], chosen.at[1, c, rows, :], odd_send.at[p, i], odd_recv.at[p, i],
                            in_plane(i)) for i in NEIGHBOURS]

    low = iota((32, 128), 1) < 64

    def second(t):
        panel = jnp.concatenate([chosen_f[h, pl.ds(t, COLS, stride=STEP), :] for h in (0, 1)], axis=0)
        turned = swap_halves(panel)
        both = jnp.concatenate(
            [jnp.where(low, panel, 0.0), jnp.where(low, turned, 0.0),
             jnp.where(low, 0.0, turned), jnp.where(low, 0.0, panel)], axis=0).astype(BF)
        out_f[pl.ds(t, T, stride=STEP), :] = dot(middle[t], both)

    for copy in even_copies:
        copy.wait()
    for i in range(COLS):
        chosen_f[0, i * STEP:i * STEP + T, :] = chosen[0, i].astype(F32)
    for p in range(PARTS):
        for copy in odd_copies[p * 15:(p + 1) * 15]:
            copy.wait()
        for i in range(COLS):
            chosen_f[1, i * STEP + p * PART:i * STEP + (p + 1) * PART, :] = (
                chosen[1, i, p * PART:(p + 1) * PART, :].astype(F32))
        pl.loop(p * PART, (p + 1) * PART, unroll=16)(second)
        for x in range(64):
            out[p * PART:(p + 1) * PART, x * 128:(x + 1) * 128] = (
                out_f[x * STEP + p * PART:x * STEP + (p + 1) * PART, :].astype(BF))


def on_device(tensor, occ_panels, virt_panels, b_owner, b_local):
    hbm = pl.BlockSpec(memory_space=pltpu.HBM)
    operands = (tensor, occ_panels, virt_panels, b_owner.T, b_local.T)
    operands = [pltpu.with_memory_space_constraint(operand, pltpu.HBM) for operand in operands]
    dma = pltpu.SemaphoreType.DMA
    return pl.pallas_call(
        kernel,
        out_shape=pltpu.VMEM((T, 8192), BF),
        in_specs=[hbm] * 5,
        out_specs=pl.BlockSpec(memory_space=pltpu.VMEM),
        scratch_shapes=[
            pltpu.VMEM((1, T), I32),
            pltpu.VMEM((2, T), I32),
            pltpu.SMEM((2, T), I32),
            pltpu.VMEM((1, 8192), BF),
            pltpu.VMEM((1, 4096), BF),
            pltpu.VMEM((64, 128), F32),
            pltpu.VMEM((T, 4096), BF),
            pltpu.VMEM((33 * STEP, 128), F32),
            pltpu.VMEM((COLS, 64, 128), BF),
            pltpu.VMEM((COLS, 128, 64), BF),
            pltpu.VMEM((T, 64, 128), BF),
            pltpu.VMEM((COLS, 2, 128), F32),
            pltpu.VMEM((COLS, 2, 128), F32),
            pltpu.VMEM((2, 128, 128), BF),
            pltpu.VMEM((ENTRIES, 128), BF),
            pltpu.VMEM((ENTRIES, 128), BF),
            pltpu.VMEM((2, ENTRIES, 128), BF),
            pltpu.VMEM((2, PADDED, 128), BF),
            pltpu.VMEM((2, COLS, T, 128), BF),
            pltpu.VMEM((2, (COLS + 1) * STEP, 128), F32),
            pltpu.VMEM((65 * STEP, 128), F32),
            dma((6,)), pltpu.SemaphoreType.REGULAR((4,)),
            dma((COLS,)), dma((COLS,)), dma((COLS,)), dma((COLS,)),
            dma((2, 5)), dma((2, 5)), dma((SERVED,)), dma((SERVED,)),
            dma((2, SERVED)), dma((2, SERVED)),
            dma((COLS,)), dma((COLS,)), dma((PARTS, COLS)), dma((PARTS, COLS)),
        ],
        compiler_params=pltpu.CompilerParams(
            collective_id=0, has_side_effects=True, vmem_limit_bytes=32 << 20),
        cost_estimate=pl.CostEstimate(flops=300_000_000, bytes_accessed=3_000_000, transcendentals=0),
    )(*operands)


def solution(mesh):
    placed = (
        P("row", "col"),
        P(("row", "col"), None),
        P(("row", "col"), None),
        P("row", None),
        P("row", None),
    )
    return jax.shard_map(
        on_device, mesh=mesh, in_specs=placed, out_specs=P("row", "col"), check_vma=False
    )
```
